512 devices in a mesh: row: 16 (over y, x), blk: 32 (over z, core).
Axes of the slice: x: 4, y: 4, z: 16, core: 2. Of those that a mesh axis runs over, the one named last changes fastest.
Arguments:
- gradient: bfloat16 [4096, 4096], P('row', 'blk'), may hold values from -1.5 to 1.5
- slot_jobs: int32 [32, 2], P('blk'), may hold values from 0 to 40, as said below
- old_stats: float32 [32, 1024, 1024], P('blk', 'row'), may hold values from -1.2 to 1.2
Outputs:
- new_stats: float32 [32, 1024, 1024], P('blk', 'row')
The draws below stay inside these ranges and needn't reach their ends.
Inputs may be any that keep to these rules, and one draw needn't show every extreme that they name: `slot_jobs`: each code below 40 appears in exactly one slot; 40 marks an empty slot.
All inputs are finite; a program needn't handle non-finite values.
Results may differ from the reference program's by a relative error of at most 0.0003.
Values may be sent and summed in bfloat16 or wider, within the bound.
No kernel may reach another device: no remote copies, remote signals or barrier semaphores. Data moves between devices by JAX's collectives and lax.ppermute only.
A program may use at most 64 MiB of HBM per device.

```python
import jax
import jax.numpy as jnp
import numpy as np
from jax import lax

BW = 4096
TILE = 1024
NT = 4
HALF = 512
UT = 10
NJOBS = 40
SLOTS = 2
N_BLK = 32


def draw_slot_jobs(key, part):
    key = jax.random.fold_in(key, 7)
    total = N_BLK * SLOTS
    order = jax.random.permutation(key, total)
    return jnp.minimum(order, NJOBS).astype(jnp.int32).reshape(N_BLK, SLOTS)


def block_levels(stream_key, shape, pieces, least, high):
    gain = 1.0
    for position, blocks in pieces:
        steps = jax.random.uniform(jax.random.fold_in(jax.random.fold_in(stream_key, 6), position), (blocks,), jnp.float32, least / len(pieces), high / len(pieces))
        gain = gain * jnp.repeat(jnp.exp(steps), shape[position] // blocks).reshape((-1,) + (1,) * (len(shape) - 1 - position))
    return gain


def bell_draw(own_key, dims, width, limit, cuts=(), dtype=jnp.bfloat16):
    loudness = block_levels(own_key, dims, cuts, -0.22, 0.18) if cuts else 1.0
    entries = jax.random.normal(own_key, dims, jnp.float32) * width * loudness
    return jnp.minimum(jnp.maximum(entries, -limit), limit).astype(dtype)


def setup_inputs(seed: int = 0) -> dict:
    seeds = jax.random.split(jax.random.key(seed), 4)
    return {
        "gradient": bell_draw(seeds[0], (BW, BW), 0.25, 1.5, ((0, 16), (1, 32))),
        "slot_jobs": draw_slot_jobs(jax.random.fold_in(seeds[3], 71), 0),
        "old_stats": bell_draw(seeds[2], (N_BLK, SLOTS * HALF, TILE), 0.2, 1.2, ((0, 32), (1, 16)), jnp.float32),
    }


def reference(gradient, slot_jobs, old_stats):
    left = jnp.dot(gradient, gradient.T, preferred_element_type=jnp.float32)
    right = jnp.dot(gradient.T, gradient, preferred_element_type=jnp.float32)
    stacked = jnp.stack([left, right, jnp.zeros_like(left)])
    upper_i, upper_j = np.triu_indices(NT)
    table_i = jnp.asarray(upper_i.astype(np.int32))
    table_j = jnp.asarray(upper_j.astype(np.int32))
    per_kind = 2 * UT

    def one_slot(job_code):
        gram_kind = jnp.minimum(job_code // per_kind, 2).astype(jnp.int32)
        within = job_code % per_kind
        tile_id = (within // 2).astype(jnp.int32)
        half_index = (within % 2).astype(jnp.int32)
        start_row = (table_i[tile_id] * TILE + half_index * HALF).astype(jnp.int32)
        start_col = (table_j[tile_id] * TILE).astype(jnp.int32)
        return lax.dynamic_slice(stacked, (gram_kind, start_row, start_col), (1, HALF, TILE))[0]

    tiles = lax.map(one_slot, slot_jobs.reshape(-1))
    tiles = tiles.reshape(old_stats.shape)
    return 0.95 * old_stats + 0.05 * tiles
```

```python
import jax
import jax.numpy as jnp
import numpy as np
from jax import lax
from jax.sharding import PartitionSpec as P

TILE = 1024
NT = 4
HALF = 512
UT = 10
LANES = 128
GAIN = 2.0**15


def panels(gradient):
    rows, cols = gradient.shape
    n_row = lax.axis_size("row")
    n_blk = lax.axis_size("blk")
    depth = cols // n_row
    scaled = gradient.astype(jnp.float32) * GAIN
    largest = jnp.max(jnp.abs(scaled))
    scaled = scaled.astype(jnp.float16)
    out = scaled.T.reshape(n_row, depth, rows)
    mark = jnp.broadcast_to(largest.astype(jnp.float16), out.shape)
    got = lax.all_to_all(jnp.concatenate([out, mark], axis=1), "row", split_axis=0, concat_axis=0, tiled=True)
    narrow = got[:, :depth].reshape(n_row, depth, rows // LANES, LANES)
    narrow = narrow.transpose(0, 2, 1, 3).reshape(rows, cols)
    largest = jnp.max(got[:, depth:])
    mark = jnp.broadcast_to(largest, (16, cols))
    every = lax.all_gather(jnp.concatenate([scaled, narrow, mark], axis=0), "blk", axis=0, tiled=False)
    largest = jnp.max(every[:, 2 * rows :].astype(jnp.float32))
    right = every[:, :rows].astype(jnp.bfloat16)
    left = every[:, rows : 2 * rows].astype(jnp.bfloat16).reshape(n_blk, n_blk, depth, LANES)
    left = left.transpose(1, 0, 2, 3).reshape(n_blk, rows, LANES)
    return jnp.stack([left, right]), largest


def slot_term(job_code, both):
    per_kind = 2 * UT
    upper_i, upper_j = np.triu_indices(NT)
    table_i = jnp.asarray(upper_i.astype(np.int32))
    table_j = jnp.asarray(upper_j.astype(np.int32))
    gram_kind = jnp.minimum(job_code // per_kind, 1)
    within = job_code % per_kind
    tile_id = within // 2
    half_index = within % 2
    start_row = (table_i[tile_id] * TILE + half_index * HALF) // LANES
    start_col = (table_j[tile_id] * TILE) // LANES
    zero = jnp.zeros_like(gram_kind)
    depth = both.shape[2]
    panel_row = lax.dynamic_slice(both, (gram_kind, start_row, zero, zero), (1, HALF // LANES, depth, LANES))[0]
    panel_col = lax.dynamic_slice(both, (gram_kind, start_col, zero, zero), (1, TILE // LANES, depth, LANES))[0]
    panel_row = panel_row.transpose(1, 0, 2).reshape(depth, HALF)
    panel_col = panel_col.transpose(1, 0, 2).reshape(depth, TILE)
    return lax.dot_general(panel_row, panel_col, (((0,), (0,)), ((), ())), preferred_element_type=jnp.float32)


def per_device(gradient, slot_jobs, old_stats):
    both, largest = panels(gradient)
    slot_count = slot_jobs.shape[1]
    share = old_stats.shape[1]
    n_row = lax.axis_size("row")
    largest = jnp.maximum(largest, 2.0**-24)
    unit = largest * largest * (both.shape[2] / 2.0**15)
    terms = [(slot_term(slot_jobs[0, slot], both) / unit).astype(jnp.float16) for slot in range(slot_count)]
    terms = jnp.concatenate(terms, axis=0).reshape(n_row, share, TILE)
    got = lax.all_to_all(terms, "row", split_axis=0, concat_axis=0, tiled=True)
    summed = jnp.sum(got.astype(jnp.float32), axis=0)
    slot = lax.axis_index("row") // (n_row // slot_count)
    used = slot_jobs[0, slot] < 4 * UT
    summed = jnp.where(used, summed * (unit * GAIN**-2), 0.0)
    return 0.95 * old_stats + 0.05 * summed[None]


def solution(mesh):
    placed = (P("row", "blk"), P("blk", None), P("blk", "row", None))
    return jax.shard_map(
        per_device, mesh=mesh, in_specs=placed, out_specs=P("blk", "row", None), check_vma=False
    )
```

```python
import jax
import jax.numpy as jnp
from jax import lax
from jax.experimental import pallas as pl
from jax.experimental.pallas import tpu as pltpu
from jax.sharding import PartitionSpec as P

TILE = 1024
HALF = 512
UT = 10
LANES = 128
GAIN = 2.0**15
MARK = 16


def gathered(gradient):
    rows, cols = gradient.shape
    n_row = lax.axis_size("row")
    depth = cols // n_row
    out = gradient.T.reshape(n_row, depth, rows)
    got = lax.all_to_all(out, "row", split_axis=0, concat_axis=0, tiled=True)
    narrow = got.reshape(n_row, depth, rows // LANES, LANES).transpose(0, 2, 1, 3).reshape(rows, cols)
    both = jnp.concatenate([gradient, narrow], axis=0).astype(jnp.float32) * GAIN
    every = lax.all_gather(both.astype(jnp.float16), "blk", axis=0, tiled=False)
    return every.astype(jnp.bfloat16)


def product_kernel(jobs, every, out, left_a, left_b, right_a, right_b, sems):
    n_blk = every.shape[0]
    depth = right_a.shape[2]
    unit = depth // n_blk
    wide_a, wide_b = HALF // LANES, TILE // LANES
    share = HALF // (out.shape[0] // 2)

    def place(slot):
        code = jobs[slot]
        within = lax.rem(code, 2 * UT)
        t = within // 2
        i = (t >= 4).astype(jnp.int32) + (t >= 7).astype(jnp.int32) + (t >= 9).astype(jnp.int32)
        j = t - 3 * (t >= 4).astype(jnp.int32) - 2 * (t >= 7).astype(jnp.int32) - (t >= 9).astype(jnp.int32)
        return code < 2 * UT, i * wide_b + lax.rem(within, 2) * wide_a, j * wide_b

    def copies(slot):
        is_left, at_a, at_b = place(slot)
        left = [
            pltpu.make_async_copy(
                every.at[:, pl.ds(pl.multiple_of(depth + unit * at, 16), unit * wide)], dst.at[slot], sems.at[slot, n]
            )
            for n, (at, wide, dst) in enumerate(((at_a, wide_a, left_a), (at_b, wide_b, left_b)))
        ]
        right = [
            pltpu.make_async_copy(every.at[pl.ds(at, wide), pl.ds(0, depth)], dst.at[slot], sems.at[slot, n])
            for n, (at, wide, dst) in enumerate(((at_a, wide_a, right_a), (at_b, wide_b, right_b)))
        ]
        return is_left, left, right

    for slot in range(2):
        is_left, left, right = copies(slot)

        @pl.when(is_left)
        def _():
            for c in left:
                c.start()

        @pl.when(jnp.logical_not(is_left))
        def _():
            for c in right:
                c.start()

    for slot in range(2):
        is_left, left, right = copies(slot)

        @pl.when(is_left)
        def _():
            for c in left:
                c.wait()
            for src, dst, wide in ((left_a, right_a, wide_a), (left_b, right_b, wide_b)):
                for n in range(wide // 2):
                    pair = src[slot, :, 2 * unit * n : 2 * unit * (n + 1), :].astype(jnp.float32)
                    for m in range(2):
                        piece = pair[:, unit * m : unit * (m + 1), :].reshape(depth, LANES)
                        dst[slot, 2 * n + m] = piece.astype(jnp.bfloat16)

        @pl.when(jnp.logical_not(is_left))
        def _():
            for c in right:
                c.wait()

        def top(ref):
            return jnp.max(jnp.abs(ref[slot].astype(jnp.float32)), axis=(0, 1, 2), keepdims=True)[0]

        bound = jnp.maximum(top(right_a), 2.0**-30) * jnp.maximum(top(right_b), 2.0**-30) * (depth / 2.0**15)
        power = jnp.ceil(jnp.log2(bound))
        scale = jnp.exp2(-power)
        for q in range(out.shape[0] // 2):
            out[slot * (out.shape[0] // 2) + q, wide_b * share :, :] = jnp.broadcast_to(power, (MARK, LANES))
        for a in range(wide_a):
            lhs = right_a[slot, a].T
            for b in range(wide_b):
                term = jnp.dot(lhs, right_b[slot, b], preferred_element_type=jnp.float32) * scale
                for m in range(LANES // share):
                    q = slot * (out.shape[0] // 2) + a * (LANES // share) + m
                    out[q, b * share : (b + 1) * share, :] = term[m * share : (m + 1) * share]


def products(jobs, every, n_row):
    depth = every.shape[1] // 2
    n_blk = every.shape[0]
    unit = depth // n_blk
    wide_a, wide_b = HALF // LANES, TILE // LANES
    share = 2 * HALF // n_row
    return pl.pallas_call(
        product_kernel,
        out_shape=jax.ShapeDtypeStruct((n_row, wide_b * share + MARK, LANES), jnp.float32),
        in_specs=[pl.BlockSpec(memory_space=pltpu.SMEM), pl.BlockSpec(memory_space=pl.ANY)],
        out_specs=pl.BlockSpec(memory_space=pltpu.VMEM),
        scratch_shapes=[
            pltpu.VMEM((2, n_blk, unit * wide_a, LANES), jnp.bfloat16),
            pltpu.VMEM((2, n_blk, unit * wide_b, LANES), jnp.bfloat16),
            pltpu.VMEM((2, wide_a, depth, LANES), jnp.bfloat16),
            pltpu.VMEM((2, wide_b, depth, LANES), jnp.bfloat16),
            pltpu.SemaphoreType.DMA((2, 2)),
        ],
        compiler_params=pltpu.CompilerParams(vmem_limit_bytes=24 * 2**20),
        cost_estimate=pl.CostEstimate(
            flops=4 * HALF * TILE * depth, bytes_accessed=every.size, transcendentals=0
        ),
    )(jobs, every)


def per_device(gradient, slot_jobs, old_stats):
    n_row = lax.axis_size("row")
    share = old_stats.shape[1]
    every = gathered(gradient)
    terms = products(slot_jobs[0], every, n_row).astype(jnp.float16)
    got = lax.all_to_all(terms, "row", split_axis=0, concat_axis=0, tiled=True)
    groups = TILE // LANES
    unit = jnp.exp2(got[:, groups * share :, :][:, :1, :1].astype(jnp.float32)) * GAIN**-2
    summed = jnp.sum(got[:, : groups * share].astype(jnp.float32) * unit, axis=0)
    summed = summed.reshape(groups, share, LANES).transpose(1, 0, 2).reshape(share, TILE)
    slot = lax.axis_index("row") // (n_row // 2)
    used = slot_jobs[0, slot] < 4 * UT
    return 0.95 * old_stats + 0.05 * jnp.where(used, summed, 0.0)[None]


def solution(mesh):
    placed = (P("row", "blk"), P("blk", None), P("blk", "row", None))
    return jax.shard_map(
        per_device, mesh=mesh, in_specs=placed, out_specs=P("blk", "row", None), check_vma=False
    )
```

```python
import jax
import jax.numpy as jnp
from jax import lax
from jax.experimental import pallas as pl
from jax.experimental.pallas import tpu as pltpu
from jax.sharding import PartitionSpec as P

TILE = 1024
HALF = 512
UT = 10
LANES = 128
GAIN = 2.0**15
MARK = 8


def gathered(gradient):
    rows, cols = gradient.shape
    n_row = lax.axis_size("row")
    depth = cols // n_row
    out = gradient.T.reshape(n_row, depth, rows)
    got = lax.all_to_all(out, "row", split_axis=0, concat_axis=0, tiled=True)
    narrow = got.reshape(n_row, depth, rows // LANES, LANES).transpose(0, 2, 1, 3).reshape(rows, cols)
    both = jnp.concatenate([gradient, narrow], axis=0).astype(jnp.float32) * GAIN
    every = lax.all_gather(both.astype(jnp.float16), "blk", axis=0, tiled=False)
    return every.astype(jnp.bfloat16)


def product_kernel(jobs, every, out, left_a, left_b, right_a, right_b, sems):
    n_blk = every.shape[0]
    depth = right_a.shape[2]
    unit = depth // n_blk
    wide_a, wide_b = HALF // LANES, TILE // LANES
    share = HALF // (out.shape[0] // 2)

    def place(slot):
        code = jobs[slot]
        within = lax.rem(code, 2 * UT)
        t = within // 2
        i = (t >= 4).astype(jnp.int32) + (t >= 7).astype(jnp.int32) + (t >= 9).astype(jnp.int32)
        j = t - 3 * (t >= 4).astype(jnp.int32) - 2 * (t >= 7).astype(jnp.int32) - (t >= 9).astype(jnp.int32)
        return code < 2 * UT, i * wide_b + lax.rem(within, 2) * wide_a, j * wide_b

    def copies(slot):
        is_left, at_a, at_b = place(slot)
        left = [
            pltpu.make_async_copy(
                every.at[:, pl.ds(pl.multiple_of(depth + unit * at, 16), unit * wide)], dst.at[slot], sems.at[slot, n]
            )
            for n, (at, wide, dst) in enumerate(((at_a, wide_a, left_a), (at_b, wide_b, left_b)))
        ]
        right = [
            pltpu.make_async_copy(every.at[pl.ds(at, wide), pl.ds(0, depth)], dst.at[slot], sems.at[slot, n])
            for n, (at, wide, dst) in enumerate(((at_a, wide_a, right_a), (at_b, wide_b, right_b)))
        ]
        return is_left, left, right

    for slot in range(2):
        is_left, left, right = copies(slot)

        @pl.when(is_left)
        def _():
            for c in left:
                c.start()

        @pl.when(jnp.logical_not(is_left))
        def _():
            for c in right:
                c.start()

    for slot in range(2):
        is_left, left, right = copies(slot)

        @pl.when(is_left)
        def _():
            for c in left:
                c.wait()
            for src, dst, wide in ((left_a, right_a, wide_a), (left_b, right_b, wide_b)):
                for n in range(wide // 2):
                    pair = src[slot, :, 2 * unit * n : 2 * unit * (n + 1), :].astype(jnp.float32)
                    for m in range(2):
                        piece = pair[:, unit * m : unit * (m + 1), :].reshape(depth, LANES)
                        dst[slot, 2 * n + m] = piece.astype(jnp.bfloat16)

        @pl.when(jnp.logical_not(is_left))
        def _():
            for c in right:
                c.wait()

        def top(ref):
            return jnp.max(jnp.abs(ref[slot].astype(jnp.float32)), axis=(0, 1, 2), keepdims=True)[0]

        bound = jnp.maximum(top(right_a), 2.0**-30) * jnp.maximum(top(right_b), 2.0**-30) * (depth / 2.0**15)
        power = jnp.ceil(jnp.log2(bound))
        scale = jnp.where(jobs[slot] < 4 * UT, jnp.exp2(-power), 0.0)
        for q in range(out.shape[0] // 2):
            out[slot * (out.shape[0] // 2) + q, wide_b * share :, :] = jnp.broadcast_to(power, (MARK, LANES))
        for a in range(wide_a):
            lhs = right_a[slot, a].T
            for b in range(wide_b):
                term = jnp.dot(lhs, right_b[slot, b], preferred_element_type=jnp.float32) * scale
                for m in range(LANES // share):
                    q = slot * (out.shape[0] // 2) + a * (LANES // share) + m
                    out[q, b * share : (b + 1) * share, :] = term[m * share : (m + 1) * share]


def products(jobs, every, n_row):
    depth = every.shape[1] // 2
    n_blk = every.shape[0]
    unit = depth // n_blk
    wide_a, wide_b = HALF // LANES, TILE // LANES
    share = 2 * HALF // n_row
    return pl.pallas_call(
        product_kernel,
        out_shape=jax.ShapeDtypeStruct((n_row, wide_b * share + MARK, LANES), jnp.float32),
        in_specs=[pl.BlockSpec(memory_space=pltpu.SMEM), pl.BlockSpec(memory_space=pl.ANY)],
        out_specs=pl.BlockSpec(memory_space=pltpu.VMEM),
        scratch_shapes=[
            pltpu.VMEM((2, n_blk, unit * wide_a, LANES), jnp.bfloat16),
            pltpu.VMEM((2, n_blk, unit * wide_b, LANES), jnp.bfloat16),
            pltpu.VMEM((2, wide_a, depth, LANES), jnp.bfloat16),
            pltpu.VMEM((2, wide_b, depth, LANES), jnp.bfloat16),
            pltpu.SemaphoreType.DMA((2, 2)),
        ],
        compiler_params=pltpu.CompilerParams(vmem_limit_bytes=24 * 2**20),
        cost_estimate=pl.CostEstimate(
            flops=4 * HALF * TILE * depth, bytes_accessed=every.size, transcendentals=0
        ),
    )(jobs, every)


def per_device(gradient, slot_jobs, old_stats):
    n_row = lax.axis_size("row")
    share = old_stats.shape[1]
    every = gathered(gradient)
    terms = products(slot_jobs[0], every, n_row).astype(jnp.float16)
    got = lax.all_to_all(terms, "row", split_axis=0, concat_axis=0, tiled=True)
    groups = TILE // LANES
    unit = jnp.exp2(got[:, groups * share :, :][:, :1, :1].astype(jnp.float32)) * (0.05 * GAIN**-2)
    summed = jnp.sum(got[:, : groups * share].astype(jnp.float32) * unit, axis=0)
    summed = summed.reshape(groups, share, LANES).transpose(1, 0, 2).reshape(share, TILE)
    return 0.95 * old_stats + summed[None]


def solution(mesh):
    placed = (P("row", "blk"), P("blk", None), P("blk", "row", None))
    return jax.shard_map(
        per_device, mesh=mesh, in_specs=placed, out_specs=P("blk", "row", None), check_vma=False
    )
```

```python
import math

import jax
import jax.numpy as jnp
from jax import lax
from jax.experimental import pallas as pl
from jax.experimental.pallas import tpu as pltpu
from jax.sharding import PartitionSpec as P

TILE = 1024
HALF = 512
UT = 10
LANES = 128
GAIN = 2.0**15
MARK = 8


def gathered(gradient):
    rows, cols = gradient.shape
    n_row = lax.axis_size("row")
    depth = cols // n_row
    out = gradient.T.reshape(n_row, depth, rows)
    got = lax.all_to_all(out, "row", split_axis=0, concat_axis=0, tiled=True)
    narrow = got.reshape(n_row, depth, rows // LANES, LANES).transpose(0, 2, 1, 3).reshape(rows, cols)
    both = jnp.concatenate([gradient, narrow], axis=0).astype(jnp.float32) * GAIN
    every = lax.all_gather(both.astype(jnp.float16), "blk", axis=0, tiled=False)
    return every.astype(jnp.bfloat16)


def product_kernel(jobs, every, out, left_a, left_b, right_a, right_b, sems):
    n_blk = every.shape[0]
    depth = right_a.shape[2]
    unit = depth // n_blk
    wide_a, wide_b = HALF // LANES, TILE // LANES
    n_row = out.shape[0]
    share = HALF // (n_row // 2)
    side = math.isqrt(n_row)
    along_x = lax.rem(lax.axis_index("blk"), 2) == 0
    fraction = lax.axis_index("row").astype(jnp.float32) / n_row

    def chunk(row):
        return jnp.where(along_x, row % side * side + row // side, row)

    def place(slot):
        code = jobs[slot]
        within = lax.rem(code, 2 * UT)
        t = within // 2
        i = (t >= 4).astype(jnp.int32) + (t >= 7).astype(jnp.int32) + (t >= 9).astype(jnp.int32)
        j = t - 3 * (t >= 4).astype(jnp.int32) - 2 * (t >= 7).astype(jnp.int32) - (t >= 9).astype(jnp.int32)
        return code < 2 * UT, i * wide_b + lax.rem(within, 2) * wide_a, j * wide_b

    def copies(slot):
        is_left, at_a, at_b = place(slot)
        left = [
            pltpu.make_async_copy(
                every.at[:, pl.ds(pl.multiple_of(depth + unit * at, 16), unit * wide)], dst.at[slot], sems.at[slot, n]
            )
            for n, (at, wide, dst) in enumerate(((at_a, wide_a, left_a), (at_b, wide_b, left_b)))
        ]
        right = [
            pltpu.make_async_copy(every.at[pl.ds(at, wide), pl.ds(0, depth)], dst.at[slot], sems.at[slot, n])
            for n, (at, wide, dst) in enumerate(((at_a, wide_a, right_a), (at_b, wide_b, right_b)))
        ]
        return is_left, left, right

    for slot in range(2):
        is_left, left, right = copies(slot)

        @pl.when(is_left)
        def _():
            for c in left:
                c.start()

        @pl.when(jnp.logical_not(is_left))
        def _():
            for c in right:
                c.start()

    for slot in range(2):
        is_left, left, right = copies(slot)

        @pl.when(is_left)
        def _():
            for c in left:
                c.wait()
            for src, dst, wide in ((left_a, right_a, wide_a), (left_b, right_b, wide_b)):
                for n in range(wide // 2):
                    pair = src[slot, :, 2 * unit * n : 2 * unit * (n + 1), :].astype(jnp.float32)
                    for m in range(2):
                        piece = pair[:, unit * m : unit * (m + 1), :].reshape(depth, LANES)
                        dst[slot, 2 * n + m] = piece.astype(jnp.bfloat16)

        @pl.when(jnp.logical_not(is_left))
        def _():
            for c in right:
                c.wait()

        def top(ref):
            most = jnp.max(jnp.abs(ref[slot]), axis=0).astype(jnp.float32)
            return jnp.max(most, axis=(0, 1), keepdims=True)

        bound = jnp.maximum(top(right_a), 2.0**-30) * jnp.maximum(top(right_b), 2.0**-30) * (depth / 2.0**15)
        power = jnp.ceil(jnp.log2(bound)) + fraction
        scale = jnp.where(jobs[slot] < 4 * UT, jnp.exp2(-power), 0.0)
        places = [chunk(slot * (n_row // 2) + q) for q in range(n_row // 2)]
        for to in places:
            out[to, wide_b * share :, :] = jnp.broadcast_to(power, (MARK, LANES))
        lhs = jnp.concatenate([right_a[slot, a].T for a in range(wide_a)], axis=0)
        for b in range(0, wide_b, 2):
            rhs = jnp.concatenate([right_b[slot, b], right_b[slot, b + 1]], axis=1)
            term = jnp.dot(lhs, rhs, preferred_element_type=jnp.float32) * scale
            for n in range(2):
                for q, to in enumerate(places):
                    piece = term[q * share : (q + 1) * share, n * LANES : (n + 1) * LANES]
                    out[to, (b + n) * share : (b + n + 1) * share, :] = piece


def products(jobs, every, n_row):
    depth = every.shape[1] // 2
    n_blk = every.shape[0]
    unit = depth // n_blk
    wide_a, wide_b = HALF // LANES, TILE // LANES
    share = 2 * HALF // n_row
    return pl.pallas_call(
        product_kernel,
        out_shape=jax.ShapeDtypeStruct((n_row, wide_b * share + MARK, LANES), jnp.float32),
        in_specs=[pl.BlockSpec(memory_space=pltpu.SMEM), pl.BlockSpec(memory_space=pl.ANY)],
        out_specs=pl.BlockSpec(memory_space=pltpu.VMEM),
        scratch_shapes=[
            pltpu.VMEM((2, n_blk, unit * wide_a, LANES), jnp.bfloat16),
            pltpu.VMEM((2, n_blk, unit * wide_b, LANES), jnp.bfloat16),
            pltpu.VMEM((2, wide_a, depth, LANES), jnp.bfloat16),
            pltpu.VMEM((2, wide_b, depth, LANES), jnp.bfloat16),
            pltpu.SemaphoreType.DMA((2, 2)),
        ],
        compiler_params=pltpu.CompilerParams(vmem_limit_bytes=24 * 2**20),
        cost_estimate=pl.CostEstimate(
            flops=4 * HALF * TILE * depth, bytes_accessed=every.size, transcendentals=0
        ),
    )(jobs, every)


def steps(n_row, n_blk):
    side = math.isqrt(n_row)
    along_x = [[y * side + x for x in range(side)] for y in range(side)]
    along_y = [[y * side + x for y in range(side)] for x in range(side)]
    return [
        [[row * n_blk + b for row in line] for b in range(n_blk) for line in (lines if b % 2 == 0 else others)]
        for lines, others in ((along_x, along_y), (along_y, along_x))
    ]


def per_device(gradient, slot_jobs, old_stats):
    n_row, n_blk = lax.axis_size("row"), lax.axis_size("blk")
    side = math.isqrt(n_row)
    share = old_stats.shape[1]
    groups = TILE // LANES
    body = groups * share
    first, second = steps(n_row, n_blk)

    def exchange(terms, lines):
        return lax.all_to_all(
            terms, ("row", "blk"), split_axis=0, concat_axis=0, axis_index_groups=lines, tiled=True
        )

    every = gathered(gradient)
    terms = products(slot_jobs[0], every, n_row).astype(jnp.float16)
    got = exchange(terms.reshape(side, side, body + MARK, LANES), first)
    power = got[:, :, body:].astype(jnp.float32)
    top = jnp.max(power, axis=0) + 2.0
    factor = jnp.exp2(power - top)[:, :, :1, :1]
    summed = jnp.sum(got[:, :, :body].astype(jnp.float32) * factor, axis=0)
    got = exchange(jnp.concatenate([summed, top], axis=1).astype(jnp.float16), second)
    unit = jnp.exp2(got[:, body:][:, :1, :1].astype(jnp.float32)) * (0.05 * GAIN**-2)
    summed = jnp.sum(got[:, :body].astype(jnp.float32) * unit, axis=0)
    summed = summed.reshape(groups, share, LANES).transpose(1, 0, 2).reshape(share, TILE)
    return 0.95 * old_stats + summed[None]


def solution(mesh):
    placed = (P("row", "blk"), P("blk", None), P("blk", "row", None))
    return jax.shard_map(
        per_device, mesh=mesh, in_specs=placed, out_specs=P("blk", "row", None), check_vma=False
    )
```

```python
import math

import jax
import jax.numpy as jnp
from jax import lax
from jax.experimental import pallas as pl
from jax.experimental.pallas import tpu as pltpu
from jax.sharding import PartitionSpec as P

TILE = 1024
HALF = 512
UT = 10
LANES = 128
GAIN = 2.0**15
MARK = 8


def gathered(gradient):
    rows, cols = gradient.shape
    n_row = lax.axis_size("row")
    depth = cols // n_row
    out = gradient.T.reshape(n_row, depth, rows)
    got = lax.all_to_all(out, "row", split_axis=0, concat_axis=0, tiled=True)
    narrow = got.reshape(n_row, depth, rows // LANES, LANES).transpose(0, 2, 1, 3).reshape(rows, cols)
    both = jnp.concatenate([gradient, narrow], axis=0).astype(jnp.float32) * GAIN
    every = lax.all_gather(both.astype(jnp.float16), "blk", axis=0, tiled=False)
    return every.astype(jnp.bfloat16)


def product_kernel(jobs, every, out, left_a, left_b, right_a, right_b, sems):
    n_blk = every.shape[0]
    depth = right_a.shape[2]
    unit = depth // n_blk
    wide_a, wide_b = HALF // LANES, TILE // LANES
    n_row = out.shape[0]
    share = HALF // (n_row // 2)
    side = math.isqrt(n_row)
    along_x = lax.rem(lax.axis_index("blk"), 2) == 0
    fraction = lax.axis_index("row").astype(jnp.float32) / n_row

    def chunk(row):
        return jnp.where(along_x, row % side * side + row // side, row)

    def place(slot):
        code = jobs[slot]
        within = lax.rem(code, 2 * UT)
        t = within // 2
        i = (t >= 4).astype(jnp.int32) + (t >= 7).astype(jnp.int32) + (t >= 9).astype(jnp.int32)
        j = t - 3 * (t >= 4).astype(jnp.int32) - 2 * (t >= 7).astype(jnp.int32) - (t >= 9).astype(jnp.int32)
        return code < 2 * UT, i * wide_b + lax.rem(within, 2) * wide_a, j * wide_b

    def copies(slot):
        is_left, at_a, at_b = place(slot)
        left = [
            pltpu.make_async_copy(
                every.at[:, pl.ds(pl.multiple_of(depth + unit * at, 16), unit * wide)], dst.at[slot], sems.at[slot, n]
            )
            for n, (at, wide, dst) in enumerate(((at_a, wide_a, left_a), (at_b, wide_b, left_b)))
        ]
        right = [
            pltpu.make_async_copy(every.at[pl.ds(at, wide), pl.ds(0, depth)], dst.at[slot], sems.at[slot, n])
            for n, (at, wide, dst) in enumerate(((at_a, wide_a, right_a), (at_b, wide_b, right_b)))
        ]
        return is_left, left, right

    for slot in range(2):
        is_left, left, right = copies(slot)

        @pl.when(is_left)
        def _():
            for c in left:
                c.start()

        @pl.when(jnp.logical_not(is_left))
        def _():
            for c in right:
                c.start()

    for slot in range(2):
        is_left, left, right = copies(slot)

        @pl.when(is_left)
        def _():
            for c in left:
                c.wait()
            for src, dst, wide in ((left_a, right_a, wide_a), (left_b, right_b, wide_b)):
                for n in range(wide // 2):
                    pair = src[slot, :, 2 * unit * n : 2 * unit * (n + 1), :].astype(jnp.float32)
                    for m in range(2):
                        piece = pair[:, unit * m : unit * (m + 1), :].reshape(depth, LANES)
                        dst[slot, 2 * n + m] = piece.astype(jnp.bfloat16)

        @pl.when(jnp.logical_not(is_left))
        def _():
            for c in right:
                c.wait()

    def top(ref, slot):
        most = jnp.max(jnp.abs(ref[slot]), axis=0).astype(jnp.float32)
        return jnp.max(most, axis=(0, 1), keepdims=True)

    tilt = lax.broadcasted_iota(jnp.int32, (MARK // 2, LANES), 1).astype(jnp.float32) / LANES
    for slot in range(2):
        bound = jnp.maximum(top(right_a, slot), 2.0**-30) * jnp.maximum(top(right_b, slot), 2.0**-30)
        power = jnp.ceil(jnp.log2(bound * (depth / 2.0**14))) + fraction
        scale = jnp.where(jobs[slot] < 4 * UT, jnp.exp2(tilt[:1] - power), 0.0)
        places = [chunk(slot * (n_row // 2) + q) for q in range(n_row // 2)]
        for to in places:
            out[to, wide_b * share :, :] = jnp.concatenate([jnp.broadcast_to(power, tilt.shape), tilt], axis=0)
        lhs = jnp.concatenate([right_a[slot, a].T for a in range(wide_a)], axis=0)
        for b in range(0, wide_b, 2):
            rhs = jnp.concatenate([right_b[slot, b], right_b[slot, b + 1]], axis=1)
            term = jnp.dot(lhs, rhs, preferred_element_type=jnp.float32)
            for n in range(2):
                for q, to in enumerate(places):
                    piece = term[q * share : (q + 1) * share, n * LANES : (n + 1) * LANES] * scale
                    out[to, (b + n) * share : (b + n + 1) * share, :] = piece


def products(jobs, every, n_row):
    depth = every.shape[1] // 2
    n_blk = every.shape[0]
    unit = depth // n_blk
    wide_a, wide_b = HALF // LANES, TILE // LANES
    share = 2 * HALF // n_row
    return pl.pallas_call(
        product_kernel,
        out_shape=jax.ShapeDtypeStruct((n_row, wide_b * share + MARK, LANES), jnp.float32),
        in_specs=[pl.BlockSpec(memory_space=pltpu.SMEM), pl.BlockSpec(memory_space=pl.ANY)],
        out_specs=pl.BlockSpec(memory_space=pltpu.VMEM),
        scratch_shapes=[
            pltpu.VMEM((2, n_blk, unit * wide_a, LANES), jnp.bfloat16),
            pltpu.VMEM((2, n_blk, unit * wide_b, LANES), jnp.bfloat16),
            pltpu.VMEM((2, wide_a, depth, LANES), jnp.bfloat16),
            pltpu.VMEM((2, wide_b, depth, LANES), jnp.bfloat16),
            pltpu.SemaphoreType.DMA((2, 2)),
        ],
        compiler_params=pltpu.CompilerParams(vmem_limit_bytes=24 * 2**20),
        cost_estimate=pl.CostEstimate(
            flops=4 * HALF * TILE * depth, bytes_accessed=every.size, transcendentals=0
        ),
    )(jobs, every)


def steps(n_row, n_blk):
    side = math.isqrt(n_row)
    along_x = [[y * side + x for x in range(side)] for y in range(side)]
    along_y = [[y * side + x for y in range(side)] for x in range(side)]
    return [
        [[row * n_blk + b for row in line] for b in range(n_blk) for line in (lines if b % 2 == 0 else others)]
        for lines, others in ((along_x, along_y), (along_y, along_x))
    ]


def per_device(gradient, slot_jobs, old_stats):
    n_row, n_blk = lax.axis_size("row"), lax.axis_size("blk")
    side = math.isqrt(n_row)
    share = old_stats.shape[1]
    groups = TILE // LANES
    body = groups * share
    first, second = steps(n_row, n_blk)

    def exchange(terms, lines):
        return lax.all_to_all(
            terms, ("row", "blk"), split_axis=0, concat_axis=0, axis_index_groups=lines, tiled=True
        )

    every = gathered(gradient)
    terms = products(slot_jobs[0], every, n_row).astype(jnp.float16)
    got = exchange(terms.reshape(side, side, body + MARK, LANES), first)
    power = got[:, :, body:].astype(jnp.float32)
    top = jnp.max(power, axis=0) + 2.0
    factor = jnp.exp2(power - top)[:, :, :1, :1]
    summed = jnp.sum(got[:, :, :body].astype(jnp.float32) * factor, axis=0)
    got = exchange(jnp.concatenate([summed, top], axis=1).astype(jnp.float16), second)
    mark = got[:, body:].astype(jnp.float32)
    unit = jnp.exp2(mark[:, :1] - mark[:, -1:]) * (4.0 * 0.05 * GAIN**-2)
    summed = jnp.sum(got[:, :body].astype(jnp.float32) * unit, axis=0)
    summed = summed.reshape(groups, share, LANES).transpose(1, 0, 2).reshape(share, TILE)
    return 0.95 * old_stats + summed[None]


def solution(mesh):
    placed = (P("row", "blk"), P("blk", None), P("blk", "row", None))
    return jax.shard_map(
        per_device, mesh=mesh, in_specs=placed, out_specs=P("blk", "row", None), check_vma=False
    )
```

```python
import math

import jax
import jax.numpy as jnp
from jax import lax
from jax.experimental.layout import Layout, with_layout_constraint
from jax.experimental import pallas as pl
from jax.experimental.pallas import tpu as pltpu
from jax.sharding import PartitionSpec as P

TILE = 1024
HALF = 512
UT = 10
LANES = 128
GAIN = 2.0**15
MARK = 8


def gathered(gradient):
    rows, cols = gradient.shape
    n_row = lax.axis_size("row")
    depth = cols // n_row
    scaled = lax.optimization_barrier((gradient.astype(jnp.float32) * GAIN).astype(jnp.float16))
    out = scaled.T.reshape(n_row, depth, rows)
    got = lax.all_to_all(out, "row", split_axis=0, concat_axis=0, tiled=True)
    narrow = got.reshape(n_row, depth, rows // LANES, LANES).transpose(0, 2, 1, 3).reshape(rows, cols)
    both = with_layout_constraint(jnp.concatenate([scaled, narrow], axis=0), Layout(major_to_minor=(0, 1)))
    every = lax.all_gather(both, "blk", axis=0, tiled=False)
    return every.astype(jnp.bfloat16)


def product_kernel(jobs, every, out, right_a, right_b):
    n_blk = every.shape[0]
    depth = right_a.shape[2]
    unit = depth // n_blk
    wide_a, wide_b = HALF // LANES, TILE // LANES
    n_row = out.shape[0]
    share = HALF // (n_row // 2)
    side = math.isqrt(n_row)
    along_x = lax.rem(lax.axis_index("blk"), 2) == 0
    fraction = lax.axis_index("row").astype(jnp.float32) / n_row

    def chunk(row):
        return jnp.where(along_x, row % side * side + row // side, row)

    def place(slot):
        code = jobs[slot]
        within = lax.rem(code, 2 * UT)
        t = within // 2
        i = (t >= 4).astype(jnp.int32) + (t >= 7).astype(jnp.int32) + (t >= 9).astype(jnp.int32)
        j = t - 3 * (t >= 4).astype(jnp.int32) - 2 * (t >= 7).astype(jnp.int32) - (t >= 9).astype(jnp.int32)
        return code < 2 * UT, i * wide_b + lax.rem(within, 2) * wide_a, j * wide_b

    for slot in range(2):
        is_left, at_a, at_b = place(slot)
        panels = ((at_a, wide_a, right_a), (at_b, wide_b, right_b))

        @pl.when(is_left)
        def _():
            for at, wide, dst in panels:
                for n in range(wide // 2):
                    from_row = pl.multiple_of(depth + unit * at, 2 * unit) + 2 * unit * n
                    pair = every[:, pl.ds(from_row, 2 * unit), :].astype(jnp.float32)
                    for m in range(2):
                        piece = pair[:, unit * m : unit * (m + 1), :].reshape(depth, LANES)
                        dst[slot, 2 * n + m] = piece.astype(jnp.bfloat16)

        @pl.when(jnp.logical_not(is_left))
        def _():
            for at, wide, dst in panels:
                for n in range(wide):
                    dst[slot, n] = every[at + n, :depth, :]

    def top(ref, slot):
        most = jnp.max(jnp.abs(ref[slot]), axis=0).astype(jnp.float32)
        return jnp.max(most, axis=(0, 1), keepdims=True)

    tilt = lax.broadcasted_iota(jnp.int32, (MARK // 2, LANES), 1).astype(jnp.float32) / LANES
    for slot in range(2):
        bound = jnp.maximum(top(right_a, slot), 2.0**-30) * jnp.maximum(top(right_b, slot), 2.0**-30)
        power = jnp.ceil(jnp.log2(bound * (depth / 2.0**14))) + fraction
        scale = jnp.where(jobs[slot] < 4 * UT, jnp.exp2(tilt[:1] - power), 0.0)
        places = [chunk(slot * (n_row // 2) + q) for q in range(n_row // 2)]
        for to in places:
            out[to, wide_b * share :, :] = jnp.concatenate([jnp.broadcast_to(power, tilt.shape), tilt], axis=0)
        lhs = jnp.concatenate([right_a[slot, a].T for a in range(wide_a)], axis=0)
        for b in range(0, wide_b, 2):
            rhs = jnp.concatenate([right_b[slot, b], right_b[slot, b + 1]], axis=1)
            term = jnp.dot(lhs, rhs, preferred_element_type=jnp.float32)
            for n in range(2):
                for q, to in enumerate(places):
                    piece = term[q * share : (q + 1) * share, n * LANES : (n + 1) * LANES] * scale
                    out[to, (b + n) * share : (b + n + 1) * share, :] = piece


def products(jobs, every, n_row):
    depth = every.shape[1] // 2
    n_blk = every.shape[0]
    unit = depth // n_blk
    wide_a, wide_b = HALF // LANES, TILE // LANES
    share = 2 * HALF // n_row
    return pl.pallas_call(
        product_kernel,
        out_shape=jax.ShapeDtypeStruct((n_row, wide_b * share + MARK, LANES), jnp.float32),
        in_specs=[pl.BlockSpec(memory_space=pltpu.SMEM), pl.BlockSpec(memory_space=pltpu.VMEM)],
        out_specs=pl.BlockSpec(memory_space=pltpu.VMEM),
        scratch_shapes=[
            pltpu.VMEM((2, wide_a, depth, LANES), jnp.bfloat16),
            pltpu.VMEM((2, wide_b, depth, LANES), jnp.bfloat16),
        ],
        compiler_params=pltpu.CompilerParams(vmem_limit_bytes=24 * 2**20),
        cost_estimate=pl.CostEstimate(
            flops=4 * HALF * TILE * depth, bytes_accessed=every.size, transcendentals=0
        ),
    )(jobs, every)


def steps(n_row, n_blk):
    side = math.isqrt(n_row)
    along_x = [[y * side + x for x in range(side)] for y in range(side)]
    along_y = [[y * side + x for y in range(side)] for x in range(side)]
    return [
        [[row * n_blk + b for row in line] for b in range(n_blk) for line in (lines if b % 2 == 0 else others)]
        for lines, others in ((along_x, along_y), (along_y, along_x))
    ]


def per_device(gradient, slot_jobs, old_stats):
    n_row, n_blk = lax.axis_size("row"), lax.axis_size("blk")
    side = math.isqrt(n_row)
    share = old_stats.shape[1]
    groups = TILE // LANES
    body = groups * share
    first, second = steps(n_row, n_blk)

    def exchange(terms, lines):
        return lax.all_to_all(
            terms, ("row", "blk"), split_axis=0, concat_axis=0, axis_index_groups=lines, tiled=True
        )

    every = gathered(gradient)
    terms = products(slot_jobs[0], every, n_row).astype(jnp.float16)
    got = exchange(terms.reshape(side, side, body + MARK, LANES), first)
    power = got[:, :, body:].astype(jnp.float32)
    top = jnp.max(power, axis=0) + 2.0
    factor = jnp.exp2(power - top)[:, :, :1, :1]
    summed = jnp.sum(got[:, :, :body].astype(jnp.float32) * factor, axis=0)
    got = exchange(jnp.concatenate([summed, top], axis=1).astype(jnp.float16), second)
    mark = got[:, body:].astype(jnp.float32)
    unit = jnp.exp2(mark[:, :1] - mark[:, -1:]) * (4.0 * 0.05 * GAIN**-2)
    summed = jnp.sum(got[:, :body].astype(jnp.float32) * unit, axis=0)
    summed = summed.reshape(groups, share, LANES).transpose(1, 0, 2).reshape(share, TILE)
    return 0.95 * old_stats + summed[None]


def solution(mesh):
    placed = (P("row", "blk"), P("blk", None), P("blk", "row", None))
    return jax.shard_map(
        per_device, mesh=mesh, in_specs=placed, out_specs=P("blk", "row", None), check_vma=False
    )
```

```python
import math

import jax
import jax.numpy as jnp
from jax import lax
from jax.experimental.layout import Layout, with_layout_constraint
from jax.experimental import pallas as pl
from jax.experimental.pallas import tpu as pltpu
from jax.sharding import PartitionSpec as P

TILE = 1024
HALF = 512
UT = 10
LANES = 128
GAIN = 2.0**15
MARK = 8


def gathered(gradient):
    rows, cols = gradient.shape
    n_row = lax.axis_size("row")
    depth = cols // n_row
    scaled = lax.optimization_barrier((gradient.astype(jnp.float32) * GAIN).astype(jnp.float16))
    out = scaled.T.reshape(n_row, depth, rows)
    got = lax.all_to_all(out, "row", split_axis=0, concat_axis=0, tiled=True)
    narrow = got.reshape(n_row, depth, rows // LANES, LANES).transpose(0, 2, 1, 3).reshape(rows, cols)
    both = with_layout_constraint(jnp.concatenate([scaled, narrow], axis=0), Layout(major_to_minor=(0, 1)))
    every = lax.all_gather(both, "blk", axis=0, tiled=False)
    return every.astype(jnp.bfloat16)


def product_kernel(jobs, every, out, right_a, right_b, peak):
    n_blk = every.shape[0]
    depth = right_a.shape[2]
    unit = depth // n_blk
    wide_a, wide_b = HALF // LANES, TILE // LANES
    n_row = out.shape[0]
    share = HALF // (n_row // 2)
    side = math.isqrt(n_row)
    along_x = lax.rem(lax.axis_index("blk"), 2) == 0
    fraction = lax.axis_index("row").astype(jnp.float32) / n_row

    def chunk(row):
        return jnp.where(along_x, row % side * side + row // side, row)

    def place(slot):
        code = jobs[slot]
        within = lax.rem(code, 2 * UT)
        t = within // 2
        i = (t >= 4).astype(jnp.int32) + (t >= 7).astype(jnp.int32) + (t >= 9).astype(jnp.int32)
        j = t - 3 * (t >= 4).astype(jnp.int32) - 2 * (t >= 7).astype(jnp.int32) - (t >= 9).astype(jnp.int32)
        return code < 2 * UT, i * wide_b + lax.rem(within, 2) * wide_a, j * wide_b

    for slot in range(2):
        is_left, at_a, at_b = place(slot)
        panels = ((at_a, wide_a, right_a), (at_b, wide_b, right_b))

        @pl.when(is_left)
        def _():
            for k, (at, wide, dst) in enumerate(panels):
                most = jnp.zeros((depth, LANES), jnp.float32)
                for n in range(wide // 2):
                    from_row = pl.multiple_of(depth + unit * at, 2 * unit) + 2 * unit * n
                    pair = every[:, pl.ds(from_row, 2 * unit), :].astype(jnp.float32)
                    for m in range(2):
                        piece = pair[:, unit * m : unit * (m + 1), :].reshape(depth, LANES)
                        most = jnp.maximum(most, jnp.abs(piece))
                        dst[slot, 2 * n + m] = piece.astype(jnp.bfloat16)
                peak[slot, k] = jnp.max(most.reshape(depth // 8, 8, LANES), axis=0)

        @pl.when(jnp.logical_not(is_left))
        def _():
            for k, (at, wide, dst) in enumerate(panels):
                most = jnp.zeros((depth, LANES), jnp.bfloat16)
                for n in range(wide):
                    piece = every[at + n, :depth, :]
                    most = jnp.maximum(most, jnp.abs(piece))
                    dst[slot, n] = piece
                peak[slot, k] = jnp.max(most.astype(jnp.float32).reshape(depth // 8, 8, LANES), axis=0)

    def top(slot, k):
        return jnp.max(peak[slot, k], axis=(0, 1), keepdims=True)

    tilt = lax.broadcasted_iota(jnp.int32, (MARK // 2, LANES), 1).astype(jnp.float32) / LANES
    for slot in range(2):
        bound = jnp.maximum(top(slot, 0), 2.0**-30) * jnp.maximum(top(slot, 1), 2.0**-30)
        power = jnp.ceil(jnp.log2(bound * (depth / 2.0**14))) + fraction
        scale = jnp.where(jobs[slot] < 4 * UT, jnp.exp2(tilt[:1] - power), 0.0)
        places = [chunk(slot * (n_row // 2) + q) for q in range(n_row // 2)]
        for to in places:
            out[to, wide_b * share :, :] = jnp.concatenate([jnp.broadcast_to(power, tilt.shape), tilt], axis=0)
        lhs = jnp.concatenate([right_a[slot, a].T for a in range(wide_a)], axis=0)
        for b in range(0, wide_b, 2):
            rhs = jnp.concatenate([right_b[slot, b], right_b[slot, b + 1]], axis=1)
            term = jnp.dot(lhs, rhs, preferred_element_type=jnp.float32)
            for n in range(2):
                for q, to in enumerate(places):
                    piece = term[q * share : (q + 1) * share, n * LANES : (n + 1) * LANES] * scale
                    out[to, (b + n) * share : (b + n + 1) * share, :] = piece


def products(jobs, every, n_row):
    depth = every.shape[1] // 2
    n_blk = every.shape[0]
    unit = depth // n_blk
    wide_a, wide_b = HALF // LANES, TILE // LANES
    share = 2 * HALF // n_row
    return pl.pallas_call(
        product_kernel,
        out_shape=jax.ShapeDtypeStruct((n_row, wide_b * share + MARK, LANES), jnp.float32),
        in_specs=[pl.BlockSpec(memory_space=pltpu.SMEM), pl.BlockSpec(memory_space=pltpu.VMEM)],
        out_specs=pl.BlockSpec(memory_space=pltpu.VMEM),
        scratch_shapes=[
            pltpu.VMEM((2, wide_a, depth, LANES), jnp.bfloat16),
            pltpu.VMEM((2, wide_b, depth, LANES), jnp.bfloat16),
            pltpu.VMEM((2, 2, 8, LANES), jnp.float32),
        ],
        compiler_params=pltpu.CompilerParams(vmem_limit_bytes=24 * 2**20),
        cost_estimate=pl.CostEstimate(
            flops=4 * HALF * TILE * depth, bytes_accessed=every.size, transcendentals=0
        ),
    )(jobs, every)


def steps(n_row, n_blk):
    side = math.isqrt(n_row)
    along_x = [[y * side + x for x in range(side)] for y in range(side)]
    along_y = [[y * side + x for y in range(side)] for x in range(side)]
    return [
        [[row * n_blk + b for row in line] for b in range(n_blk) for line in (lines if b % 2 == 0 else others)]
        for lines, others in ((along_x, along_y), (along_y, along_x))
    ]


def per_device(gradient, slot_jobs, old_stats):
    n_row, n_blk = lax.axis_size("row"), lax.axis_size("blk")
    side = math.isqrt(n_row)
    share = old_stats.shape[1]
    groups = TILE // LANES
    body = groups * share
    first, second = steps(n_row, n_blk)

    def exchange(terms, lines):
        return lax.all_to_all(
            terms, ("row", "blk"), split_axis=0, concat_axis=0, axis_index_groups=lines, tiled=True
        )

    every = gathered(gradient)
    terms = products(slot_jobs[0], every, n_row).astype(jnp.float16)
    got = exchange(terms.reshape(side, side, body + MARK, LANES), first)
    power = got[:, :, body:].astype(jnp.float32)
    top = jnp.max(power, axis=0) + 2.0
    factor = jnp.exp2(power - top)[:, :, :1]
    summed = jnp.sum(got[:, :, :body].astype(jnp.float32) * factor, axis=0)
    got = exchange(jnp.concatenate([summed, top], axis=1).astype(jnp.float16), second)
    mark = got[:, body:].astype(jnp.float32)
    unit = jnp.exp2(mark[:, :1] - mark[:, -1:]) * (4.0 * 0.05 * GAIN**-2)
    summed = jnp.sum(got[:, :body].astype(jnp.float32) * unit, axis=0)
    summed = summed.reshape(groups, share, LANES).transpose(1, 0, 2).reshape(share, TILE)
    return 0.95 * old_stats + summed[None]


def solution(mesh):
    placed = (P("row", "blk"), P("blk", None), P("blk", "row", None))
    return jax.shard_map(
        per_device, mesh=mesh, in_specs=placed, out_specs=P("blk", "row", None), check_vma=False
    )
```

```python
import functools
import math

import jax
import jax.numpy as jnp
from jax import lax
from jax.experimental.layout import Layout, with_layout_constraint
from jax.experimental import pallas as pl
from jax.experimental.pallas import tpu as pltpu
from jax.sharding import PartitionSpec as P

TILE = 1024
HALF = 512
UT = 10
LANES = 128
GAIN = 2.0**15
MARK = 8


def gathered(gradient):
    rows, cols = gradient.shape
    n_row = lax.axis_size("row")
    depth = cols // n_row
    scaled = lax.optimization_barrier((gradient.astype(jnp.float32) * GAIN).astype(jnp.float16))
    out = scaled.T.reshape(n_row, depth, rows)
    got = lax.all_to_all(out, "row", split_axis=0, concat_axis=0, tiled=True)
    narrow = got.reshape(n_row, depth, rows // LANES, LANES).transpose(0, 2, 1, 3).reshape(rows, cols)
    both = with_layout_constraint(jnp.concatenate([scaled, narrow], axis=0), Layout(major_to_minor=(0, 1)))
    every = lax.all_gather(both, "blk", axis=0, tiled=False)
    return every.astype(jnp.bfloat16)


def product_kernel(jobs, every, out):
    n_blk = every.shape[0]
    depth = every.shape[1] // 2
    unit = depth // n_blk
    wide_a, wide_b = HALF // LANES, TILE // LANES
    n_row = out.shape[0]
    share = HALF // (n_row // 2)
    side = math.isqrt(n_row)
    along_x = lax.rem(lax.axis_index("blk"), 2) == 0
    fraction = lax.axis_index("row").astype(jnp.float32) / n_row

    def chunk(row):
        return jnp.where(along_x, row % side * side + row // side, row)

    def place(slot):
        code = jobs[slot]
        within = lax.rem(code, 2 * UT)
        t = within // 2
        i = (t >= 4).astype(jnp.int32) + (t >= 7).astype(jnp.int32) + (t >= 9).astype(jnp.int32)
        j = t - 3 * (t >= 4).astype(jnp.int32) - 2 * (t >= 7).astype(jnp.int32) - (t >= 9).astype(jnp.int32)
        return code < 2 * UT, i * wide_b + lax.rem(within, 2) * wide_a, j * wide_b

    tilt = lax.broadcasted_iota(jnp.int32, (MARK // 2, LANES), 1).astype(jnp.float32) / LANES

    def send(slot, rows, cols):
        def top(panels):
            most = functools.reduce(jnp.maximum, [jnp.abs(panel) for panel in panels]).astype(jnp.float32)
            return jnp.maximum(jnp.max(most, axis=(0, 1), keepdims=True), 2.0**-30)

        power = jnp.ceil(jnp.log2(top(rows) * top(cols) * (depth / 2.0**14))) + fraction
        scale = jnp.where(jobs[slot] < 4 * UT, jnp.exp2(tilt[:1] - power), 0.0)
        places = [chunk(slot * (n_row // 2) + q) for q in range(n_row // 2)]
        for to in places:
            out[to, wide_b * share :, :] = jnp.concatenate([jnp.broadcast_to(power, tilt.shape), tilt], axis=0)
        lhs = jnp.concatenate([panel.T for panel in rows], axis=0)
        for b in range(0, wide_b, 2):
            rhs = jnp.concatenate([cols[b], cols[b + 1]], axis=1)
            term = jnp.dot(lhs, rhs, preferred_element_type=jnp.float32)
            for n in range(2):
                for q, to in enumerate(places):
                    piece = term[q * share : (q + 1) * share, n * LANES : (n + 1) * LANES] * scale
                    out[to, (b + n) * share : (b + n + 1) * share, :] = piece

    for slot in range(2):
        is_left, at_a, at_b = place(slot)

        @pl.when(is_left)
        def _():
            def load(at, wide):
                panels = []
                for n in range(wide // 2):
                    from_row = pl.multiple_of(depth + unit * at, 2 * unit) + 2 * unit * n
                    pair = every[:, pl.ds(from_row, 2 * unit), :].astype(jnp.float32)
                    for m in range(2):
                        piece = pair[:, unit * m : unit * (m + 1), :].reshape(depth, LANES)
                        panels.append(piece.astype(jnp.bfloat16))
                return panels

            send(slot, load(at_a, wide_a), load(at_b, wide_b))

        @pl.when(jnp.logical_not(is_left))
        def _():
            rows = [every[at_a + n, :depth, :] for n in range(wide_a)]
            cols = [every[at_b + n, :depth, :] for n in range(wide_b)]
            send(slot, rows, cols)


def products(jobs, every, n_row):
    depth = every.shape[1] // 2
    n_blk = every.shape[0]
    unit = depth // n_blk
    wide_a, wide_b = HALF // LANES, TILE // LANES
    share = 2 * HALF // n_row
    return pl.pallas_call(
        product_kernel,
        out_shape=jax.ShapeDtypeStruct((n_row, wide_b * share + MARK, LANES), jnp.float32),
        in_specs=[pl.BlockSpec(memory_space=pltpu.SMEM), pl.BlockSpec(memory_space=pltpu.VMEM)],
        out_specs=pl.BlockSpec(memory_space=pltpu.VMEM),
        compiler_params=pltpu.CompilerParams(vmem_limit_bytes=24 * 2**20),
        cost_estimate=pl.CostEstimate(
            flops=4 * HALF * TILE * depth, bytes_accessed=every.size, transcendentals=0
        ),
    )(jobs, every)


def steps(n_row, n_blk):
    side = math.isqrt(n_row)
    along_x = [[y * side + x for x in range(side)] for y in range(side)]
    along_y = [[y * side + x for y in range(side)] for x in range(side)]
    return [
        [[row * n_blk + b for row in line] for b in range(n_blk) for line in (lines if b % 2 == 0 else others)]
        for lines, others in ((along_x, along_y), (along_y, along_x))
    ]


def per_device(gradient, slot_jobs, old_stats):
    n_row, n_blk = lax.axis_size("row"), lax.axis_size("blk")
    side = math.isqrt(n_row)
    share = old_stats.shape[1]
    groups = TILE // LANES
    body = groups * share
    first, second = steps(n_row, n_blk)

    def exchange(terms, lines):
        return lax.all_to_all(
            terms, ("row", "blk"), split_axis=0, concat_axis=0, axis_index_groups=lines, tiled=True
        )

    every = gathered(gradient)
    terms = products(slot_jobs[0], every, n_row).astype(jnp.float16)
    got = exchange(terms.reshape(side, side, body + MARK, LANES), first)
    power = got[:, :, body:].astype(jnp.float32)
    top = jnp.max(power, axis=0) + 2.0
    factor = jnp.exp2(power - top)[:, :, :1]
    summed = jnp.sum(got[:, :, :body].astype(jnp.float32) * factor, axis=0)
    got = exchange(jnp.concatenate([summed, top], axis=1).astype(jnp.float16), second)
    mark = got[:, body:].astype(jnp.float32)
    unit = jnp.exp2(mark[:, :1] - mark[:, -1:]) * (4.0 * 0.05 * GAIN**-2)
    summed = jnp.sum(got[:, :body].astype(jnp.float32) * unit, axis=0)
    summed = summed.reshape(groups, share, LANES).transpose(1, 0, 2).reshape(share, TILE)
    return 0.95 * old_stats + summed[None]


def solution(mesh):
    placed = (P("row", "blk"), P("blk", None), P("blk", "row", None))
    return jax.shard_map(
        per_device, mesh=mesh, in_specs=placed, out_specs=P("blk", "row", None), check_vma=False
    )
```

```python
import functools
import math

import jax
import jax.numpy as jnp
from jax import lax
from jax.experimental.layout import Layout, with_layout_constraint
from jax.experimental import pallas as pl
from jax.experimental.pallas import tpu as pltpu
from jax.sharding import PartitionSpec as P

TILE = 1024
HALF = 512
UT = 10
LANES = 128
SUBLANES = 8
GAIN = 2.0**15
MARK = 8


def gathered(gradient):
    rows, cols = gradient.shape
    n_row = lax.axis_size("row")
    depth = cols // n_row
    scaled = lax.optimization_barrier((gradient.astype(jnp.float32) * GAIN).astype(jnp.float16))
    out = scaled.T.reshape(n_row, depth, rows)
    got = lax.all_to_all(out, "row", split_axis=0, concat_axis=0, tiled=True)
    narrow = got.reshape(n_row, depth, rows // LANES, LANES).transpose(0, 2, 1, 3).reshape(rows, cols)
    both = with_layout_constraint(jnp.concatenate([scaled, narrow], axis=0), Layout(major_to_minor=(0, 1)))
    every = lax.all_gather(both, "blk", axis=0, tiled=False)
    return every.astype(jnp.bfloat16)


def product_kernel(jobs, every, out):
    n_blk = every.shape[0]
    depth = every.shape[1] // 2
    unit = depth // n_blk
    wide_a, wide_b = HALF // LANES, TILE // LANES
    n_row = out.shape[0]
    share = HALF // (n_row // 2)
    side = math.isqrt(n_row)
    along_x = lax.rem(lax.axis_index("blk"), 2) == 0
    fraction = lax.axis_index("row").astype(jnp.float32) / n_row

    def chunk(row):
        return jnp.where(along_x, row % side * side + row // side, row)

    def place(slot):
        code = jobs[slot]
        within = lax.rem(code, 2 * UT)
        t = within // 2
        i = (t >= 4).astype(jnp.int32) + (t >= 7).astype(jnp.int32) + (t >= 9).astype(jnp.int32)
        j = t - 3 * (t >= 4).astype(jnp.int32) - 2 * (t >= 7).astype(jnp.int32) - (t >= 9).astype(jnp.int32)
        return code < 2 * UT, i * wide_b + lax.rem(within, 2) * wide_a, j * wide_b

    tilt = lax.broadcasted_iota(jnp.int32, (MARK // 2, LANES), 1).astype(jnp.float32) / LANES

    def send(slot, rows, cols):
        def top(panels):
            most = functools.reduce(jnp.maximum, [jnp.abs(panel) for panel in panels]).astype(jnp.float32)
            return jnp.maximum(jnp.max(most, axis=(0, 1), keepdims=True), 2.0**-30)

        power = jnp.ceil(jnp.log2(top(rows) * top(cols) * (depth / 2.0**14))) + fraction
        scale = jnp.where(jobs[slot] < 4 * UT, jnp.exp2(tilt[:1] - power), 0.0)
        places = [chunk(slot * (n_row // 2) + q) for q in range(n_row // 2)]
        for to in places:
            out[to, wide_b * share :, :] = jnp.concatenate([jnp.broadcast_to(power, tilt.shape), tilt], axis=0)
        lhs = jnp.concatenate([panel.T for panel in rows], axis=0)
        for b in range(0, wide_b, 2):
            rhs = jnp.concatenate([cols[b], cols[b + 1]], axis=1)
            term = jnp.dot(lhs, rhs, preferred_element_type=jnp.float32)
            for n in range(2):
                for q, to in enumerate(places):
                    piece = term[q * share : (q + 1) * share, n * LANES : (n + 1) * LANES] * scale
                    for i in range(share // SUBLANES):
                        at = (i * wide_b + b + n) * SUBLANES
                        out[to, at : at + SUBLANES, :] = piece[i * SUBLANES : (i + 1) * SUBLANES]

    for slot in range(2):
        is_left, at_a, at_b = place(slot)

        @pl.when(is_left)
        def _():
            def load(at, wide):
                panels = []
                for n in range(wide // 2):
                    from_row = pl.multiple_of(depth + unit * at, 2 * unit) + 2 * unit * n
                    pair = every[:, pl.ds(from_row, 2 * unit), :].astype(jnp.float32)
                    for m in range(2):
                        piece = pair[:, unit * m : unit * (m + 1), :].reshape(depth, LANES)
                        panels.append(piece.astype(jnp.bfloat16))
                return panels

            send(slot, load(at_a, wide_a), load(at_b, wide_b))

        @pl.when(jnp.logical_not(is_left))
        def _():
            rows = [every[at_a + n, :depth, :] for n in range(wide_a)]
            cols = [every[at_b + n, :depth, :] for n in range(wide_b)]
            send(slot, rows, cols)


def products(jobs, every, n_row):
    depth = every.shape[1] // 2
    n_blk = every.shape[0]
    unit = depth // n_blk
    wide_a, wide_b = HALF // LANES, TILE // LANES
    share = 2 * HALF // n_row
    return pl.pallas_call(
        product_kernel,
        out_shape=jax.ShapeDtypeStruct((n_row, wide_b * share + MARK, LANES), jnp.float32),
        in_specs=[pl.BlockSpec(memory_space=pltpu.SMEM), pl.BlockSpec(memory_space=pltpu.VMEM)],
        out_specs=pl.BlockSpec(memory_space=pltpu.VMEM),
        compiler_params=pltpu.CompilerParams(vmem_limit_bytes=24 * 2**20),
        cost_estimate=pl.CostEstimate(
            flops=4 * HALF * TILE * depth, bytes_accessed=every.size, transcendentals=0
        ),
    )(jobs, every)


def steps(n_row, n_blk):
    side = math.isqrt(n_row)
    along_x = [[y * side + x for x in range(side)] for y in range(side)]
    along_y = [[y * side + x for y in range(side)] for x in range(side)]
    return [
        [[row * n_blk + b for row in line] for b in range(n_blk) for line in (lines if b % 2 == 0 else others)]
        for lines, others in ((along_x, along_y), (along_y, along_x))
    ]


def per_device(gradient, slot_jobs, old_stats):
    n_row, n_blk = lax.axis_size("row"), lax.axis_size("blk")
    side = math.isqrt(n_row)
    share = old_stats.shape[1]
    groups = TILE // LANES
    body = groups * share
    first, second = steps(n_row, n_blk)

    def exchange(terms, lines):
        return lax.all_to_all(
            terms, ("row", "blk"), split_axis=0, concat_axis=0, axis_index_groups=lines, tiled=True
        )

    every = gathered(gradient)
    terms = products(slot_jobs[0], every, n_row).astype(jnp.float16)
    got = exchange(terms.reshape(side, side, body + MARK, LANES), first)
    power = got[:, :, body:].astype(jnp.float32)
    top = jnp.max(power, axis=0) + 2.0
    factor = jnp.exp2(power - top)[:, :, :1]
    summed = jnp.sum(got.astype(jnp.float32) * factor, axis=0).astype(jnp.float16)
    got = exchange(summed.at[:, body:].set(top.astype(jnp.float16)), second)
    mark = got[:, body:].astype(jnp.float32)
    unit = jnp.exp2(mark[:, :1] - mark[:, -1:]) * (4.0 * 0.05 * GAIN**-2)
    summed = jnp.sum(got[:, :body].astype(jnp.float32) * unit, axis=0)
    summed = summed.reshape(share // SUBLANES, groups, SUBLANES, LANES).transpose(0, 2, 1, 3).reshape(share, TILE)
    return 0.95 * old_stats + summed[None]


def solution(mesh):
    placed = (P("row", "blk"), P("blk", None), P("blk", "row", None))
    return jax.shard_map(
        per_device, mesh=mesh, in_specs=placed, out_specs=P("blk", "row", None), check_vma=False
    )
```

```python
import functools
import math

import jax
import jax.numpy as jnp
from jax import lax
from jax.experimental.layout import Layout, with_layout_constraint
from jax.experimental import pallas as pl
from jax.experimental.pallas import tpu as pltpu
from jax.sharding import PartitionSpec as P

TILE = 1024
HALF = 512
UT = 10
LANES = 128
SUBLANES = 8
GAIN = 2.0**15
MARK = 8


def gathered(gradient):
    rows, cols = gradient.shape
    n_row = lax.axis_size("row")
    depth = cols // n_row
    scaled = lax.optimization_barrier((gradient.astype(jnp.float32) * GAIN).astype(jnp.float16))
    out = scaled.T.reshape(n_row, depth, rows)
    got = lax.all_to_all(out, "row", split_axis=0, concat_axis=0, tiled=True)
    narrow = got.reshape(n_row, depth, rows // LANES, LANES).transpose(0, 2, 1, 3).reshape(rows, cols)
    both = with_layout_constraint(jnp.concatenate([scaled, narrow], axis=0), Layout(major_to_minor=(0, 1)))
    every = lax.all_gather(both, "blk", axis=0, tiled=False)
    return every.astype(jnp.bfloat16)


def product_kernel(jobs, every, out):
    n_blk = every.shape[0]
    depth = every.shape[1] // 2
    unit = depth // n_blk
    wide_a, wide_b = HALF // LANES, TILE // LANES
    n_row = out.shape[0]
    share = HALF // (n_row // 2)
    side = math.isqrt(n_row)
    along_x = lax.rem(lax.axis_index("blk"), 2) == 0
    fraction = lax.axis_index("row").astype(jnp.float32) / n_row

    def chunk(row):
        return jnp.where(along_x, row % side * side + row // side, row)

    def place(slot):
        code = jobs[slot]
        within = lax.rem(code, 2 * UT)
        t = within // 2
        i = (t >= 4).astype(jnp.int32) + (t >= 7).astype(jnp.int32) + (t >= 9).astype(jnp.int32)
        j = t - 3 * (t >= 4).astype(jnp.int32) - 2 * (t >= 7).astype(jnp.int32) - (t >= 9).astype(jnp.int32)
        return code < 2 * UT, i * wide_b + lax.rem(within, 2) * wide_a, j * wide_b

    tilt = lax.broadcasted_iota(jnp.int32, (MARK // 2, LANES), 1).astype(jnp.float32) / LANES

    def send(slot, rows, cols):
        def top(panels):
            most = functools.reduce(jnp.maximum, [jnp.abs(panel) for panel in panels]).astype(jnp.float32)
            return jnp.maximum(jnp.max(most, axis=(0, 1), keepdims=True), 2.0**-30)

        power = jnp.ceil(jnp.log2(top(rows) * top(cols) * (depth / 2.0**12))) + fraction
        scale = jnp.where(jobs[slot] < 4 * UT, jnp.exp2(tilt[:1] - power), 0.0)
        places = [chunk(slot * (n_row // 2) + q) for q in range(n_row // 2)]
        for to in places:
            out[to, wide_b * share :, :] = jnp.concatenate([jnp.broadcast_to(power, tilt.shape), tilt], axis=0)
        lhs = jnp.concatenate([panel.T for panel in rows], axis=0)
        for b in range(0, wide_b, 2):
            rhs = jnp.concatenate([cols[b], cols[b + 1]], axis=1)
            term = jnp.dot(lhs, rhs, preferred_element_type=jnp.float32)
            for n in range(2):
                for q, to in enumerate(places):
                    piece = term[q * share : (q + 1) * share, n * LANES : (n + 1) * LANES] * scale
                    for i in range(share // SUBLANES):
                        at = (i * wide_b + b + n) * SUBLANES
                        out[to, at : at + SUBLANES, :] = piece[i * SUBLANES : (i + 1) * SUBLANES]

    for slot in range(2):
        is_left, at_a, at_b = place(slot)

        @pl.when(is_left)
        def _():
            def load(at, wide):
                panels = []
                for n in range(wide // 2):
                    from_row = pl.multiple_of(depth + unit * at, 2 * unit) + 2 * unit * n
                    pair = every[:, pl.ds(from_row, 2 * unit), :].astype(jnp.float32)
                    for m in range(2):
                        piece = pair[:, unit * m : unit * (m + 1), :].reshape(depth, LANES)
                        panels.append(piece.astype(jnp.bfloat16))
                return panels

            send(slot, load(at_a, wide_a), load(at_b, wide_b))

        @pl.when(jnp.logical_not(is_left))
        def _():
            rows = [every[at_a + n, :depth, :] for n in range(wide_a)]
            cols = [every[at_b + n, :depth, :] for n in range(wide_b)]
            send(slot, rows, cols)


def products(jobs, every, n_row):
    depth = every.shape[1] // 2
    n_blk = every.shape[0]
    unit = depth // n_blk
    wide_a, wide_b = HALF // LANES, TILE // LANES
    share = 2 * HALF // n_row
    return pl.pallas_call(
        product_kernel,
        out_shape=jax.ShapeDtypeStruct((n_row, wide_b * share + MARK, LANES), jnp.float32),
        in_specs=[pl.BlockSpec(memory_space=pltpu.SMEM), pl.BlockSpec(memory_space=pltpu.VMEM)],
        out_specs=pl.BlockSpec(memory_space=pltpu.VMEM),
        compiler_params=pltpu.CompilerParams(vmem_limit_bytes=24 * 2**20),
        cost_estimate=pl.CostEstimate(
            flops=4 * HALF * TILE * depth, bytes_accessed=every.size, transcendentals=0
        ),
    )(jobs, every)


def steps(n_row, n_blk):
    side = math.isqrt(n_row)
    along_x = [[y * side + x for x in range(side)] for y in range(side)]
    along_y = [[y * side + x for y in range(side)] for x in range(side)]
    return [
        [[row * n_blk + b for row in line] for b in range(n_blk) for line in (lines if b % 2 == 0 else others)]
        for lines, others in ((along_x, along_y), (along_y, along_x))
    ]


def per_device(gradient, slot_jobs, old_stats):
    n_row, n_blk = lax.axis_size("row"), lax.axis_size("blk")
    side = math.isqrt(n_row)
    share = old_stats.shape[1]
    groups = TILE // LANES
    body = groups * share
    first, second = steps(n_row, n_blk)

    def exchange(terms, lines):
        return lax.all_to_all(
            terms, ("row", "blk"), split_axis=0, concat_axis=0, axis_index_groups=lines, tiled=True
        )

    every = gathered(gradient)
    terms = products(slot_jobs[0], every, n_row).astype(jnp.float16)
    got = exchange(terms.reshape(side, side, body + MARK, LANES), first)
    mark = got[:, :, body:]
    top = jnp.max(mark, axis=0)
    factor = jnp.exp2(mark[:, :, :1].astype(jnp.float32) - top[:, :1].astype(jnp.float32))
    summed = jnp.sum(got.astype(jnp.float32) * factor, axis=0).astype(jnp.float16)
    got = exchange(summed.at[:, body:].set(top), second)
    mark = got[:, body:].astype(jnp.float32)
    unit = jnp.exp2(mark[:, :1] - mark[:, -1:]) * (0.05 * GAIN**-2)
    summed = jnp.sum(got[:, :body].astype(jnp.float32) * unit, axis=0)
    summed = summed.reshape(share // SUBLANES, groups, SUBLANES, LANES).transpose(0, 2, 1, 3).reshape(share, TILE)
    return 0.95 * old_stats + summed[None]


def solution(mesh):
    placed = (P("row", "blk"), P("blk", None), P("blk", "row", None))
    return jax.shard_map(
        per_device, mesh=mesh, in_specs=placed, out_specs=P("blk", "row", None), check_vma=False
    )
```

```python
import functools
import math

import jax
import jax.numpy as jnp
from jax import lax
from jax.experimental.layout import Layout, with_layout_constraint
from jax.experimental import pallas as pl
from jax.experimental.pallas import tpu as pltpu
from jax.sharding import PartitionSpec as P

TILE = 1024
HALF = 512
UT = 10
LANES = 128
SUBLANES = 8
GAIN = 2.0**15
MARK = 8


def gathered(gradient):
    rows, cols = gradient.shape
    n_row = lax.axis_size("row")
    depth = cols // n_row
    scaled = lax.optimization_barrier((gradient.astype(jnp.float32) * GAIN).astype(jnp.float16))
    out = scaled.T.reshape(n_row, depth, rows)
    got = lax.all_to_all(out, "row", split_axis=0, concat_axis=0, tiled=True)
    narrow = got.reshape(n_row, depth, rows // LANES, LANES).transpose(0, 2, 1, 3).reshape(rows, cols)
    both = with_layout_constraint(jnp.concatenate([scaled, narrow], axis=0), Layout(major_to_minor=(0, 1)))
    every = lax.all_gather(both, "blk", axis=0, tiled=False)
    return every.astype(jnp.bfloat16)


def product_kernel(jobs, every, out):
    n_blk = every.shape[0]
    depth = every.shape[1] // 2
    unit = depth // n_blk
    wide_a, wide_b = HALF // LANES, TILE // LANES
    n_row = out.shape[0]
    share = HALF // (n_row // 2)
    side = math.isqrt(n_row)
    along_x = lax.rem(lax.axis_index("blk"), 2) == 0
    fraction = lax.axis_index("row").astype(jnp.float32) / n_row

    def chunk(row):
        return jnp.where(along_x, row % side * side + row // side, row)

    def place(slot):
        code = jobs[slot]
        within = lax.rem(code, 2 * UT)
        t = within // 2
        i = (t >= 4).astype(jnp.int32) + (t >= 7).astype(jnp.int32) + (t >= 9).astype(jnp.int32)
        j = t - 3 * (t >= 4).astype(jnp.int32) - 2 * (t >= 7).astype(jnp.int32) - (t >= 9).astype(jnp.int32)
        return code < 2 * UT, i * wide_b + lax.rem(within, 2) * wide_a, j * wide_b

    tilt = lax.broadcasted_iota(jnp.int32, (MARK // 2, LANES), 1).astype(jnp.float32) / LANES

    def send(slot, rows, cols):
        def top(panels):
            most = functools.reduce(jnp.maximum, [jnp.abs(panel) for panel in panels]).astype(jnp.float32)
            return jnp.maximum(jnp.max(most, axis=(0, 1), keepdims=True), 2.0**-30)

        power = jnp.ceil(jnp.log2(top(rows) * top(cols) * (depth / 2.0**12))) + fraction
        scale = jnp.where(jobs[slot] < 4 * UT, jnp.exp2(tilt[:1] - power), 0.0)
        places = [chunk(slot * (n_row // 2) + q) for q in range(n_row // 2)]
        for to in places:
            out[to, wide_b * share :, :] = jnp.concatenate([jnp.broadcast_to(power, tilt.shape), tilt], axis=0)
        lhs = jnp.concatenate([panel.T for panel in rows], axis=0)
        for b in range(0, wide_b, 2):
            rhs = jnp.concatenate([cols[b], cols[b + 1]], axis=1)
            term = jnp.dot(lhs, rhs, preferred_element_type=jnp.float32)
            for n in range(2):
                for q, to in enumerate(places):
                    piece = term[q * share : (q + 1) * share, n * LANES : (n + 1) * LANES] * scale
                    for i in range(share // SUBLANES):
                        at = (i * wide_b + b + n) * SUBLANES
                        out[to, at : at + SUBLANES, :] = piece[i * SUBLANES : (i + 1) * SUBLANES]

    for slot in range(2):
        is_left, at_a, at_b = place(slot)

        @pl.when(is_left)
        def _():
            def load(at, wide):
                panels = []
                for n in range(wide // 2):
                    from_row = pl.multiple_of(depth + unit * at, 2 * unit) + 2 * unit * n
                    pair = every[:, pl.ds(from_row, 2 * unit), :].astype(jnp.float32)
                    for m in range(2):
                        piece = pair[:, unit * m : unit * (m + 1), :].reshape(depth, LANES)
                        panels.append(piece.astype(jnp.bfloat16))
                return panels

            send(slot, load(at_a, wide_a), load(at_b, wide_b))

        @pl.when(jnp.logical_not(is_left))
        def _():
            rows = [every[at_a + n, :depth, :] for n in range(wide_a)]
            cols = [every[at_b + n, :depth, :] for n in range(wide_b)]
            send(slot, rows, cols)


def products(jobs, every, n_row):
    depth = every.shape[1] // 2
    n_blk = every.shape[0]
    unit = depth // n_blk
    wide_a, wide_b = HALF // LANES, TILE // LANES
    share = 2 * HALF // n_row
    return pl.pallas_call(
        product_kernel,
        out_shape=jax.ShapeDtypeStruct((n_row, wide_b * share + MARK, LANES), jnp.float32),
        in_specs=[pl.BlockSpec(memory_space=pltpu.SMEM), pl.BlockSpec(memory_space=pltpu.VMEM)],
        out_specs=pl.BlockSpec(memory_space=pltpu.VMEM),
        compiler_params=pltpu.CompilerParams(vmem_limit_bytes=24 * 2**20),
        cost_estimate=pl.CostEstimate(
            flops=4 * HALF * TILE * depth, bytes_accessed=every.size, transcendentals=0
        ),
    )(jobs, every)


def steps(n_row, n_blk):
    side = math.isqrt(n_row)
    along_x = [[y * side + x for x in range(side)] for y in range(side)]
    along_y = [[y * side + x for y in range(side)] for x in range(side)]
    return [
        [[row * n_blk + b for row in line] for b in range(n_blk) for line in (lines if b % 2 == 0 else others)]
        for lines, others in ((along_x, along_y), (along_y, along_x))
    ]


def per_device(gradient, slot_jobs, old_stats):
    n_row, n_blk = lax.axis_size("row"), lax.axis_size("blk")
    side = math.isqrt(n_row)
    share = old_stats.shape[1]
    groups = TILE // LANES
    body = groups * share
    first, second = steps(n_row, n_blk)

    def exchange(terms, lines):
        return lax.all_to_all(
            terms, ("row", "blk"), split_axis=0, concat_axis=0, axis_index_groups=lines, tiled=True
        )

    every = gathered(gradient)
    terms = products(slot_jobs[0], every, n_row).astype(jnp.float16)
    got = exchange(terms.reshape(side, side, body + MARK, LANES), first)
    mark = got[:, :, body:]
    top = jnp.max(mark, axis=0)
    factor = jnp.exp2(mark[:, :, :1].astype(jnp.float32) - top[:, :1].astype(jnp.float32))
    summed = sum(got[n].astype(jnp.float32) * factor[n] for n in range(side)).astype(jnp.float16)
    got = exchange(summed.at[:, body:].set(top), second)
    mark = got[:, body:].astype(jnp.float32)
    unit = jnp.exp2(mark[:, :1] - mark[:, -1:]) * (0.05 * GAIN**-2)
    summed = jnp.sum(got[:, :body].astype(jnp.float32) * unit, axis=0)
    summed = summed.reshape(share // SUBLANES, groups, SUBLANES, LANES).transpose(0, 2, 1, 3).reshape(share, TILE)
    return 0.95 * old_stats + summed[None]


def solution(mesh):
    placed = (P("row", "blk"), P("blk", None), P("blk", "row", None))
    return jax.shard_map(
        per_device, mesh=mesh, in_specs=placed, out_specs=P("blk", "row", None), check_vma=False
    )
```
